32 devices in a mesh: row: 4 (over y, core), col: 8 (over z, x).
Axes of the slice: x: 2, y: 2, z: 4, core: 2. Of those that a mesh axis runs over, the one named last changes fastest.
Arguments:
- a_blocks: bfloat16 [2048, 4096], P(('row', 'col')), may hold values from -0.75 to 0.75
- blk_row: int32 [2048], P(('row', 'col')), may hold values from 0 to 255, as said below
- blk_col: int32 [2048], P(('row', 'col')), may hold values from 0 to 255, as said below
- drop_mask: int32 [2048], P(('row', 'col')), may hold values 0 or 1
- prolong: bfloat16 [256, 1024], P(('row', 'col')), may hold values from -6 to 6
- agg_label: int32 [256], P(('row', 'col')), may hold values from 0 to 1
- inv_diag: bfloat16 [256, 4096], P(('row', 'col'))
Outputs:
- coarse: float32 [2048, 1024], P(('row', 'col'))
The draws below stay inside these ranges and needn't reach their ends.
Inputs may be any that keep to these rules, and one draw needn't show every extreme that they name: `blk_row`: blocks stand 64 to a device, devices in row-major order over (row, col); a block on the device (r, c) has its row element in r * 64 to (r + 1) * 64 - 1. Every element is the row and column of one block. `blk_col`: A block on the device (r, c) has a column element e with (e // 8) % (size of col) = c.
All inputs are finite; a program needn't handle non-finite values. No bound on the sum of `drop_mask` on one device may be relied on, other than what follows from the above.
Results may differ from the reference program's by a relative error of at most 0.0003.
Values may be sent and summed in bfloat16 or wider, within the bound.
A program may use at most 64 MiB of HBM per device.

```python
import jax
import jax.numpy as jnp
from jax import lax

BS = 64
PC = 16
LABELS = 2
ELD = 8
SLOT = 64
ELEMS = 256
BLOCKS = 2048
N_ROW = 4
N_COL = 8
DEVICES = 32


def build_blocks(key):
    row_span = N_COL * ELD
    device_count = N_ROW * N_COL
    devices = jnp.arange(device_count, dtype=jnp.int32)
    local_ids = jnp.arange(ELD, dtype=jnp.int32)
    diagonal = devices[:, None] * ELD + local_ids[None, :]
    near_slot = jnp.arange(3 * ELD, dtype=jnp.int32) // 3
    near_row = devices[:, None] * ELD + near_slot[None, :]
    offsets = jax.random.randint(jax.random.fold_in(key, 11), (device_count, 3 * ELD), 1, max(ELD, 2))
    near_col = devices[:, None] * ELD + (near_slot[None, :] + offsets) % ELD

    def panel_order(panel):
        return jax.random.permutation(jax.random.fold_in(jax.random.fold_in(key, 12), panel), 4 * row_span).astype(jnp.int32)
    orders = jax.vmap(panel_order)(jnp.arange(N_ROW, dtype=jnp.int32))
    far_row = (jnp.arange(N_ROW, dtype=jnp.int32)[:, None] * row_span + orders // 4).reshape(device_count, 4 * ELD)
    places = jax.random.randint(jax.random.fold_in(key, 13), (device_count, 4 * ELD), 0, N_ROW * ELD)
    col_of_device = devices % N_COL
    far_col = (places // ELD * N_COL + col_of_device[:, None]) * ELD + places % ELD
    rows = jnp.concatenate([diagonal, near_row, far_row], axis=1).reshape(-1)
    cols = jnp.concatenate([diagonal, near_col, far_col], axis=1).reshape(-1)
    return (rows.astype(jnp.int32), cols.astype(jnp.int32))


def draw_blk_row(key, part):
    return build_blocks(key)[0]


def draw_blk_col(key, part):
    return build_blocks(key)[1]


def draw_inv_diag(key, part):
    first_key, second_key = jax.random.split(key)
    lower, upper, spread = (0.5, 2.0, 0.1)
    diag_values = jax.random.uniform(first_key, (ELEMS, BS), jnp.float32, lower, upper)
    off_values = jax.random.normal(second_key, (ELEMS, BS, BS), jnp.float32) * spread
    identity = jnp.eye(BS, dtype=jnp.float32)
    matrices = off_values * (1.0 - identity) + identity * diag_values[:, :, None]
    return matrices.reshape(ELEMS, BS * BS).astype(jnp.bfloat16)


def with_ends(entries, own_key, low, largest):
    dims = entries.shape
    index_at = [jax.random.randint(jax.random.fold_in(own_key, axis), (), 0, dims[axis]) for axis in range(len(dims))]
    entries = entries.at[tuple(index_at)].set(low)
    longest = dims.index(max(dims))
    index_at[longest] = (index_at[longest] + 1) % dims[longest]
    return entries.at[tuple(index_at)].set(largest)


def block_scale(own_key, extent, cuts, low, top_value):
    gain = 1.0
    for position, parts in cuts:
        heights = jax.random.uniform(jax.random.fold_in(jax.random.fold_in(own_key, 6), position), (parts,), jnp.float32, low / len(cuts), top_value / len(cuts))
        gain = gain * jnp.repeat(jnp.exp(heights), extent[position] // parts).reshape((-1,) + (1,) * (len(extent) - 1 - position))
    return gain


def centred(key, extent, deviation, reach, cuts=(), kind=jnp.bfloat16):
    loudness = block_scale(key, extent, cuts, -0.22, 0.18) if cuts else 1.0
    values = jax.random.normal(key, extent, jnp.float32) * deviation * loudness
    return jnp.minimum(jnp.maximum(values, -reach), reach).astype(kind)


def setup_inputs(seed: int = 0) -> dict:
    arg_keys = jax.random.split(jax.random.key(seed), 8)
    a_blocks = centred(arg_keys[0], (BLOCKS, BS * BS), BS ** -0.5, 0.75, ((0, 32),))
    blk_row = draw_blk_row(jax.random.fold_in(arg_keys[7], 71), 0)
    blk_col = draw_blk_col(jax.random.fold_in(arg_keys[7], 71), 0)
    drop_mask = with_ends((jax.random.randint(arg_keys[3], (BLOCKS,), 0, 3) < 2).astype(jnp.int32), jax.random.fold_in(arg_keys[3], 1), 0, 1)
    prolong = centred(arg_keys[4], (ELEMS, BS * PC), 1.0, 6.0, ((0, 32),))
    agg_label = with_ends(jax.random.randint(arg_keys[5], (ELEMS,), 0, LABELS), jax.random.fold_in(arg_keys[5], 1), 0, LABELS - 1).astype(jnp.int32)
    inv_diag = draw_inv_diag(jax.random.fold_in(arg_keys[7], 71), 0)
    return dict(a_blocks=a_blocks, blk_row=blk_row, blk_col=blk_col, drop_mask=drop_mask, prolong=prolong, agg_label=agg_label, inv_diag=inv_diag)


def reference(a_blocks, blk_row, blk_col, drop_mask, prolong, agg_label, inv_diag):
    highest = lax.Precision.HIGHEST
    keep = jnp.maximum(drop_mask, (blk_row == blk_col).astype(jnp.int32))

    def device_terms(items):
        blocks, rows, cols, keeps = items
        matrices = blocks.astype(jnp.float32).reshape(-1, BS, BS)
        col_part = prolong[cols].astype(jnp.float32).reshape(-1, BS, PC)
        row_part = prolong[rows].astype(jnp.float32).reshape(-1, BS, PC)
        keep_float = keeps.astype(jnp.float32)[:, None, None]
        kept_terms = jnp.einsum("sij,sjk->sik", matrices, col_part, precision=highest) * keep_float
        drop_terms = jnp.einsum("sij,sjk->sik", matrices, row_part, precision=highest) * (1.0 - keep_float)
        return kept_terms.reshape(-1, BS * PC), drop_terms.reshape(-1, BS * PC)

    kept_all, drop_all = lax.map(device_terms, (a_blocks.reshape(DEVICES, SLOT, BS * BS), blk_row.reshape(DEVICES, SLOT), blk_col.reshape(DEVICES, SLOT), keep.reshape(DEVICES, SLOT)))
    lumped = jax.ops.segment_sum(drop_all.reshape(BLOCKS, BS * PC), blk_row, num_segments=ELEMS)

    def device_out(items):
        kept_terms, rows, cols = items
        col_run = cols // ELD
        row_run = rows // ELD
        col_label = agg_label[cols]
        same_group = (rows[:, None] == rows[None, :]) & (col_run[:, None] == col_run[None, :]) & (col_label[:, None] == col_label[None, :])
        grouped = jnp.dot(same_group.astype(jnp.float32), kept_terms, precision=highest)
        target = ((col_run == row_run) & (col_label == agg_label[rows])).astype(jnp.float32)
        grouped = grouped + target[:, None] * lumped[rows]
        inverse = inv_diag[rows].astype(jnp.float32).reshape(-1, BS, BS)
        coarse = jnp.einsum("sij,sjk->sik", inverse, grouped.reshape(-1, BS, PC), precision=highest)
        return coarse.reshape(-1, BS * PC)

    coarse = lax.map(device_out, (kept_all, blk_row.reshape(DEVICES, SLOT), blk_col.reshape(DEVICES, SLOT)))
    return coarse.reshape(BLOCKS, BS * PC)
```

```python
import functools

import jax
import jax.numpy as jnp
from jax import lax
from jax.experimental import pallas as pl
from jax.experimental.pallas import tpu as pltpu
from jax.sharding import PartitionSpec as P

BS = 64
PC = 16
LANES = 128
MESH = pl.DeviceIdType.MESH
F32 = jnp.float32
BF16 = jnp.bfloat16


def iota(shape, dim):
    return lax.broadcasted_iota(jnp.int32, shape, dim)


def split(x):
    high = x.astype(BF16)
    return high, (x - high.astype(F32)).astype(BF16)


def dot(a, b):
    return jnp.dot(a, b, preferred_element_type=F32)


def kernel(
    n_row, n_col, row_ref, col_ref, drop_ref, label_ref, a_ref, b_ref, d_ref,
    out_ref, y_ref, t_ref, s_ref, msg_ref, inv_ref, lump_ref, in_ref, tmp_ref,
    brs, brr, bcs, bcr, ds_, dr, ls, lr_,
):
    slots = a_ref.shape[0]
    own = b_ref.shape[0]
    wide = BS * PC
    half = wide // 2
    pair = BS // 2
    chunk_a = BS * BS // LANES
    chunk_b = wide // LANES
    per_chunk = LANES // (2 * PC)
    pad = 2 * own
    me_row = lax.axis_index("row")
    me_col = lax.axis_index("col")

    def row_peer(d):
        return (lax.rem(me_row + d, n_row), me_col)

    def col_peer(d):
        return (me_row, lax.rem(me_col + d, n_col))

    barrier = pltpu.get_barrier_semaphore()
    for d in range(1, n_row):
        pl.semaphore_signal(barrier, inc=1, device_id=row_peer(d), device_id_type=MESH)
    for d in range(1, n_col):
        pl.semaphore_signal(barrier, inc=1, device_id=col_peer(d), device_id_type=MESH)

    b_all = b_ref[...]
    msg_ref[0:pad, 0:half] = jnp.concatenate([b_all[:, :half], b_all[:, half:]], axis=0)
    labels = jnp.zeros((pad, LANES), F32)
    sub = iota((pad, LANES), 0)
    for e in range(own):
        labels = jnp.where(sub == e, label_ref[e].astype(F32), labels)
    msg_ref[0:pad, half:half + LANES] = labels.astype(BF16)

    src = iota((LANES, LANES), 0)
    dst = iota((LANES, LANES), 1)
    want = dst // BS * BS + dst % pair * 2 + dst % BS // pair
    perm = (src == want).astype(BF16)
    half_a = chunk_a // 2
    for t in range(half_a):
        pieces = [dot(d_ref[:, u * LANES:(u + 1) * LANES], perm) for u in (t, t + half_a)]
        tmp_ref[pl.ds(t, own, stride=chunk_a), :] = pieces[0]
        tmp_ref[pl.ds(t + half_a, own, stride=chunk_a), :] = pieces[1]
        inv_ref[0:pad, t * LANES:(t + 1) * LANES] = (
            jnp.concatenate(pieces, axis=0).astype(BF16))

    pl.semaphore_wait(barrier, n_row + n_col - 2)

    copies = []
    for d in range(1, n_row):
        copies.append(pltpu.make_async_remote_copy(
            src_ref=msg_ref.at[pl.ds(0, pad)], dst_ref=msg_ref.at[pl.ds(d * pad, pad)],
            send_sem=brs.at[d], recv_sem=brr.at[d],
            device_id=row_peer(d), device_id_type=MESH))
    for d in range(1, n_col):
        copies.append(pltpu.make_async_remote_copy(
            src_ref=msg_ref.at[pl.ds(0, pad)],
            dst_ref=msg_ref.at[pl.ds((n_row - 1 + d) * pad, pad)],
            send_sem=bcs.at[d], recv_sem=bcr.at[d],
            device_id=col_peer(d), device_id_type=MESH))
    inv_copies = [pltpu.make_async_remote_copy(
        src_ref=inv_ref.at[pl.ds(0, pad)], dst_ref=inv_ref.at[pl.ds(d * pad, pad)],
        send_sem=ds_.at[d], recv_sem=dr.at[d],
        device_id=col_peer(d), device_id_type=MESH) for d in range(1, n_col)]
    for c in copies:
        c.start()
    for c in inv_copies:
        c.start()

    for t in range(chunk_a):
        y_ref[pl.ds(t, slots, stride=chunk_a), :] = dot(
            a_ref[:, t * LANES:(t + 1) * LANES], perm
        )

    blk_row = row_ref[...]
    blk_col = col_ref[...]
    local = blk_row - me_row * (n_col * own)
    keep = jnp.maximum(drop_ref[...], (blk_row == blk_col).astype(jnp.int32))
    keep_f = keep.astype(F32)
    col_slot = lax.rem(me_row - blk_col // (n_col * own) + n_row, n_row)
    k_col = col_slot * pad + blk_col % own
    owner = local // own
    back = lax.rem(me_col - owner + n_col, n_col)
    k_row = jnp.where(back == 0, 0, n_row - 1 + back) * pad + local % own
    l_idx = lax.rem(owner - me_col + n_col, n_col) * own + local % own
    same_run = (blk_col // own == blk_row // own).astype(F32)
    group = (local * n_row + col_slot).astype(F32)
    k_sel = jnp.where(keep == 1, k_col, k_row).astype(F32)
    sub = iota((8, slots), 0)
    packed = jnp.zeros((8, slots), F32)
    for at, v in enumerate((k_sel, k_col.astype(F32), k_row.astype(F32), group, same_run,
                            (back * pad + local % own).astype(F32))):
        packed = jnp.where(sub == at, v, packed)
    eye = (iota((slots, slots), 0) == iota((slots, slots), 1)).astype(F32)
    columns = lax.dot_general(
        eye, packed, (((1,), (1,)), ((), ())),
        precision=lax.Precision.HIGHEST, preferred_element_type=F32)
    sel_c, kcol_c, krow_c, group_c, run_c, inv_c = (
        columns[:, i:i + 1] for i in range(6))

    src = iota((LANES, per_chunk * LANES), 0)
    dst = iota((LANES, per_chunk * LANES), 1)
    fan = (src == dst // LANES * (2 * PC) + dst % (2 * PC)).astype(BF16)
    fan2 = jnp.concatenate([fan, fan], axis=0)
    lane = iota((pair, LANES), 1)
    even = lane // PC % 2 == 0

    def spread(x, fan, count):
        r = dot(x[0], fan)
        for v in range(per_chunk):
            t_ref[pl.ds(x[1] * per_chunk + v, count, stride=pair), :] = (
                r[:, v * LANES:(v + 1) * LANES])

    def multiply(b, lhs, two):
        at = pl.ds(pl.multiple_of(b * pair, pair), pair)
        g = t_ref[at, :]
        r = pltpu.roll(g, PC, 1)
        zero = jnp.zeros_like(g)
        parts = [jnp.where(even, g, zero), jnp.where(even, r, zero),
                 jnp.where(even, zero, r), jnp.where(even, zero, g)]
        x = jnp.concatenate(parts, axis=0)
        if two:
            high, low = split(x)
            s_ref[at, :] = dot(jnp.concatenate([lhs, lhs], axis=1),
                               jnp.concatenate([high, low], axis=0))
        else:
            s_ref[at, :] = dot(lhs, x.astype(BF16))

    def collect(u, count):
        place = iota((count, LANES), 1) // (2 * PC)
        z = s_ref[pl.ds(u * per_chunk, count, stride=pair), :]
        for v in range(1, per_chunk):
            z = jnp.where(
                place == v, s_ref[pl.ds(u * per_chunk + v, count, stride=pair), :], z)
        return z

    for c in copies:
        c.wait_recv()

    depth = msg_ref.shape[0]
    slot_lane = iota((slots, depth), 1).astype(F32)
    pick = jnp.concatenate(
        [(sel_c == slot_lane).astype(BF16), (sel_c + own == slot_lane).astype(BF16)], axis=0)
    chosen = dot(pick, msg_ref[:, 0:half]).astype(BF16)
    for u in range(chunk_b):
        where = u % (chunk_b // 2) * LANES
        base = u // (chunk_b // 2) * slots
        spread((chosen[base:base + slots, where:where + LANES], u), fan, slots)

    def first(b, _):
        at = pl.ds(pl.multiple_of(b * pair, pair), pair)
        multiply(b, y_ref[at, :].astype(BF16), False)
        return 0

    lax.fori_loop(0, slots, first, 0, unroll=8)

    row_lane = iota((slots, n_row * pad), 1).astype(F32)
    col_label = dot((kcol_c == row_lane).astype(BF16),
                    msg_ref[0:n_row * pad, half:half + LANES])
    own_lane = iota((slots, pad), 1).astype(F32)
    row_label = dot((krow_c == own_lane).astype(BF16), msg_ref[0:pad, half:half + LANES])
    marks = (col_label == iota((slots, LANES), 1).astype(F32)).astype(BF16)
    same_label = lax.dot_general(
        marks, marks, (((1,), (1,)), ((), ())), preferred_element_type=F32)
    same = jnp.where(group_c == group, same_label * keep_f, 0.0)
    panel = n_col * own
    dropped = jnp.where(
        iota((panel, slots), 0) == l_idx, jnp.broadcast_to(1.0 - keep_f, (panel, slots)), 0.0)
    sums = jnp.concatenate([same, dropped], axis=0)
    sums = jnp.concatenate([sums, sums], axis=1).astype(BF16)
    target = jnp.where(row_label == col_label, run_c, 0.0)[:, 0:pad]
    target = jnp.where(
        krow_c == (iota((slots, pad), 1) % own).astype(F32), target, 0.0).astype(BF16)

    grouped = []
    for u in range(chunk_b):
        high, low = split(collect(u, slots))
        r = dot(sums, jnp.concatenate([high, low], axis=0))
        lump_ref[:, u * LANES:(u + 1) * LANES] = r[slots:, :]
        grouped.append(r[:slots, :])

    lump_copies = [pltpu.make_async_remote_copy(
        src_ref=lump_ref.at[pl.ds(d * own, own)], dst_ref=in_ref.at[d],
        send_sem=ls.at[d], recv_sem=lr_.at[d],
        device_id=col_peer(d), device_id_type=MESH) for d in range(1, n_col)]
    for c in lump_copies:
        c.start()

    for u in range(chunk_b):
        spread((jnp.concatenate(split(grouped[u]), axis=1), u), fan2, slots)

    for c in inv_copies:
        c.wait_recv()

    inv_lane = iota((slots, n_col * pad), 1).astype(F32)
    pick = jnp.concatenate(
        [(inv_c == inv_lane).astype(BF16), (inv_c + own == inv_lane).astype(BF16)], axis=0)
    for t in range(half_a):
        r = dot(pick, inv_ref[:, t * LANES:(t + 1) * LANES])
        y_ref[pl.ds(t, slots, stride=chunk_a), :] = r[:slots]
        y_ref[pl.ds(t + half_a, slots, stride=chunk_a), :] = r[slots:]

    def second(b, _):
        at = pl.ds(pl.multiple_of(b * pair, pair), pair)
        multiply(b, y_ref[at, :].astype(BF16), True)
        return 0

    lax.fori_loop(0, slots, second, 0, unroll=8)
    for u in range(chunk_b):
        out_ref[:, u * LANES:(u + 1) * LANES] = collect(u, slots)

    for c in lump_copies:
        c.wait_recv()
    total = lump_ref[0:own, :]
    for d in range(1, n_col):
        total = total + in_ref[d]
    for u in range(chunk_b):
        spread((jnp.concatenate(split(total[:, u * LANES:(u + 1) * LANES]), axis=1), u),
               fan2, own)
    for e in range(own):
        multiply(e, tmp_ref[e * pair:(e + 1) * pair, :].astype(BF16), True)
    for u in range(chunk_b):
        at = slice(u * LANES, (u + 1) * LANES)
        out_ref[:, at] = out_ref[:, at] + dot(
            target, jnp.concatenate(split(collect(u, own)), axis=0))

    for c in copies + inv_copies + lump_copies:
        c.wait_send()


def body(a_blocks, blk_row, blk_col, drop_mask, prolong, agg_label, inv_diag):
    slots = a_blocks.shape[0]
    own = prolong.shape[0]
    n_row = lax.axis_size("row")
    n_col = lax.axis_size("col")
    wide = BS * PC
    vmem = pl.BlockSpec(memory_space=pltpu.VMEM)
    smem = pl.BlockSpec(memory_space=pltpu.SMEM)
    dma = pltpu.SemaphoreType.DMA
    return pl.pallas_call(
        functools.partial(kernel, n_row, n_col),
        out_shape=jax.ShapeDtypeStruct((slots, wide), F32),
        in_specs=[vmem, vmem, vmem, smem, vmem, vmem, vmem],
        out_specs=vmem,
        scratch_shapes=[
            pltpu.VMEM((slots * BS // 2, LANES), F32),
            pltpu.VMEM((slots * BS // 2, LANES), F32),
            pltpu.VMEM((slots * BS // 2, LANES), F32),
            pltpu.VMEM(((n_row + n_col - 1) * 2 * own, wide // 2 + LANES), BF16),
            pltpu.VMEM((n_col * 2 * own, BS * BS // 2), BF16),
            pltpu.VMEM((n_col * own, wide), F32),
            pltpu.VMEM((n_col, own, wide), F32),
            pltpu.VMEM((own * BS // 2, LANES), F32),
            dma((n_row,)), dma((n_row,)), dma((n_col,)), dma((n_col,)),
            dma((n_col,)), dma((n_col,)), dma((n_col,)), dma((n_col,)),
        ],
        compiler_params=pltpu.CompilerParams(
            collective_id=0, has_side_effects=True, vmem_limit_bytes=40 * 2**20),
    )(
        blk_row.reshape(1, slots), blk_col.reshape(1, slots),
        drop_mask.reshape(1, slots), agg_label, a_blocks, prolong, inv_diag,
    )


def solution(mesh):
    return jax.shard_map(
        body,
        mesh=mesh,
        in_specs=(
            P(("row", "col"), None),
            P(("row", "col")),
            P(("row", "col")),
            P(("row", "col")),
            P(("row", "col"), None),
            P(("row", "col")),
            P(("row", "col"), None),
        ),
        out_specs=P(("row", "col"), None),
        check_vma=False,
    )
```

```python
import functools

import jax
import jax.numpy as jnp
from jax import lax
from jax.experimental import pallas as pl
from jax.experimental.pallas import tpu as pltpu
from jax.sharding import PartitionSpec as P

BS = 64
PC = 16
LANES = 128
MESH = pl.DeviceIdType.MESH
F32 = jnp.float32
BF16 = jnp.bfloat16


def iota(shape, dim):
    return lax.broadcasted_iota(jnp.int32, shape, dim)


def split(x):
    high = x.astype(BF16)
    return high, (x - high.astype(F32)).astype(BF16)


def dot(a, b):
    return jnp.dot(a, b, preferred_element_type=F32)


def kernel(
    n_row, n_col, row_hbm, col_hbm, drop_hbm, label_hbm, a_hbm, b_hbm, d_hbm,
    out_ref, row_ref, col_ref, drop_ref, label_ref, a_ref, b_ref, d_ref, y_ref, t_ref, s_ref, msg_ref, inv_ref, lump_ref, in_ref, tmp_ref,
    brs, brr, bcs, bcr, ds_, dr, fs, fr, ls, lr_, loads,
):
    slots = a_ref.shape[0]
    own = b_ref.shape[0]
    wide = BS * PC
    half = wide // 2
    pair = BS // 2
    chunk_a = BS * BS // LANES
    chunk_b = wide // LANES
    per_chunk = LANES // (2 * PC)
    pad = 2 * own
    me_row = lax.axis_index("row")
    me_col = lax.axis_index("col")

    def row_peer(d):
        return (lax.rem(me_row + d, n_row), me_col)

    def col_peer(d):
        return (me_row, lax.rem(me_col + d, n_col))

    fetch = [pltpu.make_async_copy(x, y, loads.at[i]) for i, (x, y) in enumerate((
        (d_hbm, d_ref), (b_hbm, b_ref), (label_hbm, label_ref), (row_hbm, row_ref),
        (col_hbm, col_ref), (drop_hbm, drop_ref), (a_hbm, a_ref)))]
    for c in fetch:
        c.start()
    partner = me_col + 1 - 2 * lax.rem(me_col, 2)

    barrier = pltpu.get_barrier_semaphore()
    for d in range(1, n_row):
        pl.semaphore_signal(barrier, inc=1, device_id=row_peer(d), device_id_type=MESH)
    for d in range(1, n_col):
        pl.semaphore_signal(barrier, inc=1, device_id=col_peer(d), device_id_type=MESH)

    fetch[1].wait()
    fetch[2].wait()
    b_all = b_ref[...]
    msg_ref[0:pad, 0:half] = jnp.concatenate([b_all[:, :half], b_all[:, half:]], axis=0)
    mine = (iota((pad, own), 0) == iota((pad, own), 1)).astype(F32)
    labels = jnp.sum(mine * label_ref[...].astype(F32), axis=1, keepdims=True)
    msg_ref[0:pad, half:half + LANES] = jnp.broadcast_to(labels, (pad, LANES)).astype(BF16)

    src = iota((LANES, LANES), 0)
    dst = iota((LANES, LANES), 1)
    want = dst // BS * BS + dst % pair * 2 + dst % BS // pair
    perm = (src == want).astype(BF16)
    half_a = chunk_a // 2
    fetch[0].wait()
    for t in range(half_a):
        pieces = [dot(d_ref[:, u * LANES:(u + 1) * LANES], perm) for u in (t, t + half_a)]
        tmp_ref[pl.ds(t, own, stride=chunk_a), :] = pieces[0]
        tmp_ref[pl.ds(t + half_a, own, stride=chunk_a), :] = pieces[1]
        inv_ref[0:pad, t * LANES:(t + 1) * LANES] = (
            jnp.concatenate(pieces, axis=0).astype(BF16))

    pl.semaphore_wait(barrier, n_row + n_col - 2)

    copies = []
    for d in range(1, n_row):
        copies.append(pltpu.make_async_remote_copy(
            src_ref=msg_ref.at[pl.ds(0, pad)], dst_ref=msg_ref.at[pl.ds(d * pad, pad)],
            send_sem=brs.at[d], recv_sem=brr.at[d],
            device_id=row_peer(d), device_id_type=MESH))
    for d in range(1, n_col):
        copies.append(pltpu.make_async_remote_copy(
            src_ref=msg_ref.at[pl.ds(0, pad)],
            dst_ref=msg_ref.at[pl.ds((n_row - 1 + d) * pad, pad)],
            send_sem=bcs.at[d], recv_sem=bcr.at[d],
            device_id=col_peer(d), device_id_type=MESH))
    half_col = n_col // 2
    inv_copies = [pltpu.make_async_remote_copy(
        src_ref=inv_ref.at[pl.ds(0, pad)], dst_ref=inv_ref.at[pl.ds(d * pad, pad)],
        send_sem=ds_.at[d], recv_sem=dr.at[d],
        device_id=col_peer(2 * d), device_id_type=MESH) for d in range(1, half_col)]
    pass_copies = [pltpu.make_async_remote_copy(
        src_ref=inv_ref.at[pl.ds(d * pad, pad)],
        dst_ref=inv_ref.at[pl.ds((half_col + d) * pad, pad)],
        send_sem=fs.at[d], recv_sem=fr.at[d],
        device_id=(me_row, partner), device_id_type=MESH) for d in range(half_col)]
    for c in copies:
        c.start()
    for c in inv_copies:
        c.start()
    pass_copies[0].start()

    fetch[6].wait()
    for t in range(chunk_a):
        y_ref[pl.ds(t, slots, stride=chunk_a), :] = dot(
            a_ref[:, t * LANES:(t + 1) * LANES], perm
        )

    for c in fetch[3:6]:
        c.wait()
    blk_row = row_ref[...]
    blk_col = col_ref[...]
    local = blk_row - me_row * (n_col * own)
    keep = jnp.maximum(drop_ref[...], (blk_row == blk_col).astype(jnp.int32))
    keep_f = keep.astype(F32)
    col_slot = lax.rem(me_row - blk_col // (n_col * own) + n_row, n_row)
    k_col = col_slot * pad + blk_col % own
    owner = local // own
    back = lax.rem(me_col - owner + n_col, n_col)
    away = lax.rem(partner - owner + n_col, n_col)
    held = jnp.where(back % 2 == 0, back // 2, half_col + away // 2)
    k_row = jnp.where(back == 0, 0, n_row - 1 + back) * pad + local % own
    l_idx = lax.rem(owner - me_col + n_col, n_col) * own + local % own
    same_run = (blk_col // own == blk_row // own).astype(F32)
    group = (local * n_row + col_slot).astype(F32)
    k_sel = jnp.where(keep == 1, k_col, k_row).astype(F32)
    sub = iota((8, slots), 0)
    packed = jnp.zeros((8, slots), F32)
    for at, v in enumerate((k_sel, k_col.astype(F32), k_row.astype(F32), group, same_run,
                            (held * pad + local % own).astype(F32))):
        packed = jnp.where(sub == at, v, packed)
    eye = (iota((slots, slots), 0) == iota((slots, slots), 1)).astype(F32)
    columns = lax.dot_general(
        eye, packed, (((1,), (1,)), ((), ())),
        precision=lax.Precision.HIGHEST, preferred_element_type=F32)
    sel_c, kcol_c, krow_c, group_c, run_c, inv_c = (
        columns[:, i:i + 1] for i in range(6))

    src = iota((LANES, per_chunk * LANES), 0)
    dst = iota((LANES, per_chunk * LANES), 1)
    fan = (src == dst // LANES * (2 * PC) + dst % (2 * PC)).astype(BF16)
    fan2 = jnp.concatenate([fan, fan], axis=0)
    lane = iota((pair, LANES), 1)
    even = lane // PC % 2 == 0

    def spread(x, fan, count):
        r = dot(x[0], fan)
        for v in range(per_chunk):
            t_ref[pl.ds(x[1] * per_chunk + v, count, stride=pair), :] = (
                r[:, v * LANES:(v + 1) * LANES])

    def multiply(b, lhs, two):
        at = pl.ds(pl.multiple_of(b * pair, pair), pair)
        g = t_ref[at, :]
        r = pltpu.roll(g, PC, 1)
        zero = jnp.zeros_like(g)
        parts = [jnp.where(even, g, zero), jnp.where(even, r, zero),
                 jnp.where(even, zero, r), jnp.where(even, zero, g)]
        x = jnp.concatenate(parts, axis=0)
        if two:
            high, low = split(x)
            s_ref[at, :] = dot(jnp.concatenate([lhs, lhs], axis=1),
                               jnp.concatenate([high, low], axis=0))
        else:
            s_ref[at, :] = dot(lhs, x.astype(BF16))

    def collect(u, count):
        place = iota((count, LANES), 1) // (2 * PC)
        z = s_ref[pl.ds(u * per_chunk, count, stride=pair), :]
        for v in range(1, per_chunk):
            z = jnp.where(
                place == v, s_ref[pl.ds(u * per_chunk + v, count, stride=pair), :], z)
        return z

    for c in copies:
        c.wait_recv()

    depth = msg_ref.shape[0]
    slot_lane = iota((slots, depth), 1).astype(F32)
    pick = jnp.concatenate(
        [(sel_c == slot_lane).astype(BF16), (sel_c + own == slot_lane).astype(BF16)], axis=0)
    chosen = dot(pick, msg_ref[:, 0:half]).astype(BF16)
    for u in range(chunk_b):
        where = u % (chunk_b // 2) * LANES
        base = u // (chunk_b // 2) * slots
        spread((chosen[base:base + slots, where:where + LANES], u), fan, slots)

    for c, nxt in zip(inv_copies, pass_copies[1:]):
        c.wait_recv()
        nxt.start()

    def first(b, _):
        at = pl.ds(pl.multiple_of(b * pair, pair), pair)
        multiply(b, y_ref[at, :].astype(BF16), False)
        return 0

    lax.fori_loop(0, slots, first, 0, unroll=8)

    row_lane = iota((slots, n_row * pad), 1).astype(F32)
    col_label = dot((kcol_c == row_lane).astype(BF16),
                    msg_ref[0:n_row * pad, half:half + LANES])
    own_lane = iota((slots, pad), 1).astype(F32)
    row_label = dot((krow_c == own_lane).astype(BF16), msg_ref[0:pad, half:half + LANES])
    marks = (col_label == iota((slots, LANES), 1).astype(F32)).astype(BF16)
    same_label = lax.dot_general(
        marks, marks, (((1,), (1,)), ((), ())), preferred_element_type=F32)
    same = jnp.where(group_c == group, same_label * keep_f, 0.0)
    panel = n_col * own
    dropped = jnp.where(
        iota((panel, slots), 0) == l_idx, jnp.broadcast_to(1.0 - keep_f, (panel, slots)), 0.0)
    sums = jnp.concatenate([same, dropped], axis=0)
    sums = jnp.concatenate([sums, sums], axis=1).astype(BF16)
    target = jnp.where(row_label == col_label, run_c, 0.0)[:, 0:pad]
    target = jnp.where(
        krow_c == (iota((slots, pad), 1) % own).astype(F32), target, 0.0).astype(BF16)

    grouped = []
    for u in range(chunk_b):
        high, low = split(collect(u, slots))
        r = dot(sums, jnp.concatenate([high, low], axis=0))
        lump_ref[:, u * LANES:(u + 1) * LANES] = r[slots:, :]
        grouped.append(r[:slots, :])

    lump_copies = [pltpu.make_async_remote_copy(
        src_ref=lump_ref.at[pl.ds(d * own, own)], dst_ref=in_ref.at[d],
        send_sem=ls.at[d], recv_sem=lr_.at[d],
        device_id=col_peer(d), device_id_type=MESH) for d in range(1, n_col)]
    for c in lump_copies:
        c.start()

    for u in range(chunk_b):
        spread((jnp.concatenate(split(grouped[u]), axis=1), u), fan2, slots)

    for c in pass_copies:
        c.wait_recv()

    inv_lane = iota((slots, n_col * pad), 1).astype(F32)
    pick = jnp.concatenate(
        [(inv_c == inv_lane).astype(BF16), (inv_c + own == inv_lane).astype(BF16)], axis=0)
    for t in range(half_a):
        r = dot(pick, inv_ref[:, t * LANES:(t + 1) * LANES])
        y_ref[pl.ds(t, slots, stride=chunk_a), :] = r[:slots]
        y_ref[pl.ds(t + half_a, slots, stride=chunk_a), :] = r[slots:]

    def second(b, _):
        at = pl.ds(pl.multiple_of(b * pair, pair), pair)
        multiply(b, y_ref[at, :].astype(BF16), True)
        return 0

    lax.fori_loop(0, slots, second, 0, unroll=8)
    for u in range(chunk_b):
        out_ref[:, u * LANES:(u + 1) * LANES] = collect(u, slots)

    for c in lump_copies:
        c.wait_recv()
    total = lump_ref[0:own, :]
    for d in range(1, n_col):
        total = total + in_ref[d]
    for u in range(chunk_b):
        spread((jnp.concatenate(split(total[:, u * LANES:(u + 1) * LANES]), axis=1), u),
               fan2, own)
    for e in range(own):
        multiply(e, tmp_ref[e * pair:(e + 1) * pair, :].astype(BF16), True)
    for u in range(chunk_b):
        at = slice(u * LANES, (u + 1) * LANES)
        out_ref[:, at] = out_ref[:, at] + dot(
            target, jnp.concatenate(split(collect(u, own)), axis=0))

    for c in copies + inv_copies + pass_copies + lump_copies:
        c.wait_send()


def body(a_blocks, blk_row, blk_col, drop_mask, prolong, agg_label, inv_diag):
    slots = a_blocks.shape[0]
    own = prolong.shape[0]
    n_row = lax.axis_size("row")
    n_col = lax.axis_size("col")
    wide = BS * PC
    vmem = pl.BlockSpec(memory_space=pltpu.VMEM)
    hbm = pl.BlockSpec(memory_space=pltpu.HBM)
    dma = pltpu.SemaphoreType.DMA
    return pl.pallas_call(
        functools.partial(kernel, n_row, n_col),
        out_shape=jax.ShapeDtypeStruct((slots, wide), F32),
        in_specs=[hbm] * 7,
        out_specs=vmem,
        scratch_shapes=[
            pltpu.VMEM((1, slots), jnp.int32),
            pltpu.VMEM((1, slots), jnp.int32),
            pltpu.VMEM((1, slots), jnp.int32),
            pltpu.VMEM((1, own), jnp.int32),
            pltpu.VMEM(a_blocks.shape, BF16),
            pltpu.VMEM(prolong.shape, BF16),
            pltpu.VMEM(inv_diag.shape, BF16),
            pltpu.VMEM((slots * BS // 2, LANES), F32),
            pltpu.VMEM((slots * BS // 2, LANES), F32),
            pltpu.VMEM((slots * BS // 2, LANES), F32),
            pltpu.VMEM(((n_row + n_col - 1) * 2 * own, wide // 2 + LANES), BF16),
            pltpu.VMEM((n_col * 2 * own, BS * BS // 2), BF16),
            pltpu.VMEM((n_col * own, wide), F32),
            pltpu.VMEM((n_col, own, wide), F32),
            pltpu.VMEM((own * BS // 2, LANES), F32),
            dma((n_row,)), dma((n_row,)), dma((n_col,)), dma((n_col,)),
            dma((n_col,)), dma((n_col,)), dma((n_col,)), dma((n_col,)),
            dma((n_col,)), dma((n_col,)), dma((7,)),
        ],
        compiler_params=pltpu.CompilerParams(
            collective_id=0, has_side_effects=True, vmem_limit_bytes=40 * 2**20),
    )(
        blk_row.reshape(1, slots), blk_col.reshape(1, slots),
        drop_mask.reshape(1, slots), agg_label.reshape(1, own), a_blocks, prolong, inv_diag,
    )


def solution(mesh):
    return jax.shard_map(
        body,
        mesh=mesh,
        in_specs=(
            P(("row", "col"), None),
            P(("row", "col")),
            P(("row", "col")),
            P(("row", "col")),
            P(("row", "col"), None),
            P(("row", "col")),
            P(("row", "col"), None),
        ),
        out_specs=P(("row", "col"), None),
        check_vma=False,
    )
```

```python
import functools

import jax
import jax.numpy as jnp
from jax import lax
from jax.experimental import pallas as pl
from jax.experimental.pallas import tpu as pltpu
from jax.sharding import PartitionSpec as P

BS = 64
PC = 16
LANES = 128
MESH = pl.DeviceIdType.MESH
F32 = jnp.float32
BF16 = jnp.bfloat16


def iota(shape, dim):
    return lax.broadcasted_iota(jnp.int32, shape, dim)


def split(x):
    high = x.astype(BF16)
    return high, (x - high.astype(F32)).astype(BF16)


def dot(a, b):
    return jnp.dot(a, b, preferred_element_type=F32)


def kernel(
    n_row, n_col, row_hbm, col_hbm, drop_hbm, label_hbm, a_hbm, b_hbm, d_hbm,
    out_ref, row_ref, col_ref, drop_ref, label_ref, a_ref, b_ref, d_ref, y_ref, t_ref, s_ref, msg_ref, inv_ref, lump_ref, in_ref, tmp_ref,
    brs, brr, bcs, bcr, ds_, dr, fs, fr, ls, lr_, loads,
):
    slots = a_ref.shape[0]
    own = b_ref.shape[0]
    wide = BS * PC
    half = wide // 2
    pair = BS // 2
    chunk_a = BS * BS // LANES
    chunk_b = wide // LANES
    per_chunk = LANES // (2 * PC)
    pad = 2 * own
    me_row = lax.axis_index("row")
    me_col = lax.axis_index("col")

    def row_peer(d):
        return (lax.rem(me_row + d, n_row), me_col)

    def col_peer(d):
        return (me_row, lax.rem(me_col + d, n_col))

    fetch = [pltpu.make_async_copy(x, y, loads.at[i]) for i, (x, y) in enumerate((
        (d_hbm, d_ref), (b_hbm, b_ref), (label_hbm, label_ref), (row_hbm, row_ref),
        (col_hbm, col_ref), (drop_hbm, drop_ref), (a_hbm, a_ref)))]
    for c in fetch:
        c.start()
    partner = me_col + 1 - 2 * lax.rem(me_col, 2)

    barrier = pltpu.get_barrier_semaphore()
    for d in range(1, n_row):
        pl.semaphore_signal(barrier, inc=1, device_id=row_peer(d), device_id_type=MESH)
    for d in range(1, n_col):
        pl.semaphore_signal(barrier, inc=1, device_id=col_peer(d), device_id_type=MESH)

    fetch[1].wait()
    fetch[2].wait()
    b_all = b_ref[...]
    msg_ref[0:pad, 0:half] = jnp.concatenate([b_all[:, :half], b_all[:, half:]], axis=0)
    mine = (iota((pad, own), 0) == iota((pad, own), 1)).astype(F32)
    labels = jnp.sum(mine * label_ref[...].astype(F32), axis=1, keepdims=True)
    msg_ref[0:pad, half:half + LANES] = jnp.broadcast_to(labels, (pad, LANES)).astype(BF16)

    src = iota((LANES, LANES), 0)
    dst = iota((LANES, LANES), 1)
    want = dst // BS * BS + dst % pair * 2 + dst % BS // pair
    perm = (src == want).astype(BF16)
    half_a = chunk_a // 2
    fetch[0].wait()
    for t in range(half_a):
        pieces = [dot(d_ref[:, u * LANES:(u + 1) * LANES], perm) for u in (t, t + half_a)]
        tmp_ref[pl.ds(t, own, stride=chunk_a), :] = pieces[0]
        tmp_ref[pl.ds(t + half_a, own, stride=chunk_a), :] = pieces[1]
        inv_ref[0:pad, t * LANES:(t + 1) * LANES] = (
            jnp.concatenate(pieces, axis=0).astype(BF16))

    pl.semaphore_wait(barrier, n_row + n_col - 2)

    copies = []
    for d in range(1, n_row):
        copies.append(pltpu.make_async_remote_copy(
            src_ref=msg_ref.at[pl.ds(0, pad)], dst_ref=msg_ref.at[pl.ds(d * pad, pad)],
            send_sem=brs.at[d], recv_sem=brr.at[d],
            device_id=row_peer(d), device_id_type=MESH))
    for d in range(1, n_col):
        copies.append(pltpu.make_async_remote_copy(
            src_ref=msg_ref.at[pl.ds(0, pad)],
            dst_ref=msg_ref.at[pl.ds((n_row - 1 + d) * pad, pad)],
            send_sem=bcs.at[d], recv_sem=bcr.at[d],
            device_id=col_peer(d), device_id_type=MESH))
    half_col = n_col // 2
    inv_copies = [pltpu.make_async_remote_copy(
        src_ref=inv_ref.at[pl.ds(0, pad)], dst_ref=inv_ref.at[pl.ds(d * pad, pad)],
        send_sem=ds_.at[d], recv_sem=dr.at[d],
        device_id=col_peer(2 * d), device_id_type=MESH) for d in range(1, half_col)]
    pass_copies = [pltpu.make_async_remote_copy(
        src_ref=inv_ref.at[pl.ds(d * pad, pad)],
        dst_ref=inv_ref.at[pl.ds((half_col + d) * pad, pad)],
        send_sem=fs.at[d], recv_sem=fr.at[d],
        device_id=(me_row, partner), device_id_type=MESH) for d in range(half_col)]
    for c in copies:
        c.start()
    for c in inv_copies:
        c.start()
    pass_copies[0].start()

    fetch[6].wait()
    for t in range(chunk_a):
        y_ref[pl.ds(t, slots, stride=chunk_a), :] = dot(
            a_ref[:, t * LANES:(t + 1) * LANES], perm
        )

    for c in fetch[3:6]:
        c.wait()
    blk_row = row_ref[...]
    blk_col = col_ref[...]
    local = blk_row - me_row * (n_col * own)
    keep = jnp.maximum(drop_ref[...], (blk_row == blk_col).astype(jnp.int32))
    keep_f = keep.astype(F32)
    col_slot = lax.rem(me_row - blk_col // (n_col * own) + n_row, n_row)
    k_col = col_slot * pad + blk_col % own
    owner = local // own
    back = lax.rem(me_col - owner + n_col, n_col)
    away = lax.rem(partner - owner + n_col, n_col)
    held = jnp.where(back % 2 == 0, back // 2, half_col + away // 2)
    k_row = jnp.where(back == 0, 0, n_row - 1 + back) * pad + local % own
    l_idx = lax.rem(owner - me_col + n_col, n_col) * own + local % own
    same_run = (blk_col // own == blk_row // own).astype(F32)
    group = (local * n_row + col_slot).astype(F32)
    k_sel = jnp.where(keep == 1, k_col, k_row).astype(F32)
    sub = iota((8, slots), 0)
    packed = jnp.zeros((8, slots), F32)
    for at, v in enumerate((k_sel, k_col.astype(F32), k_row.astype(F32), group, same_run,
                            (held * pad + local % own).astype(F32))):
        packed = jnp.where(sub == at, v, packed)
    eye = (iota((slots, slots), 0) == iota((slots, slots), 1)).astype(F32)
    columns = lax.dot_general(
        eye, packed, (((1,), (1,)), ((), ())),
        precision=lax.Precision.HIGHEST, preferred_element_type=F32)
    sel_c, kcol_c, krow_c, group_c, run_c, inv_c = (
        columns[:, i:i + 1] for i in range(6))

    src = iota((LANES, per_chunk * LANES), 0)
    dst = iota((LANES, per_chunk * LANES), 1)
    fan = (src == dst // LANES * (2 * PC) + dst % (2 * PC)).astype(BF16)
    fan2 = jnp.concatenate([fan, fan], axis=0)
    lane = iota((pair, LANES), 1)
    even = lane // PC % 2 == 0

    def spread(x, fan, count):
        r = dot(x[0], fan)
        for v in range(per_chunk):
            t_ref[pl.ds(x[1] * per_chunk + v, count, stride=pair), :] = (
                r[:, v * LANES:(v + 1) * LANES])

    def multiply(b, lhs, two):
        at = pl.ds(pl.multiple_of(b * pair, pair), pair)
        g = t_ref[at, :]
        r = pltpu.roll(g, PC, 1)
        zero = jnp.zeros_like(g)
        parts = [jnp.where(even, g, zero), jnp.where(even, r, zero),
                 jnp.where(even, zero, r), jnp.where(even, zero, g)]
        x = jnp.concatenate(parts, axis=0)
        if two:
            high, low = split(x)
            s_ref[at, :] = dot(jnp.concatenate([lhs, lhs], axis=1),
                               jnp.concatenate([high, low], axis=0))
        else:
            s_ref[at, :] = dot(lhs, x.astype(BF16))

    def collect(u, count):
        place = iota((count, LANES), 1) // (2 * PC)
        z = s_ref[pl.ds(u * per_chunk, count, stride=pair), :]
        for v in range(1, per_chunk):
            z = jnp.where(
                place == v, s_ref[pl.ds(u * per_chunk + v, count, stride=pair), :], z)
        return z

    for c in copies:
        c.wait_recv()

    depth = msg_ref.shape[0]
    slot_lane = iota((slots, depth), 1).astype(F32)
    pick = jnp.concatenate(
        [(sel_c == slot_lane).astype(BF16), (sel_c + own == slot_lane).astype(BF16)], axis=0)
    chosen = dot(pick, msg_ref[:, 0:half]).astype(BF16)
    for u in range(chunk_b):
        where = u % (chunk_b // 2) * LANES
        base = u // (chunk_b // 2) * slots
        spread((chosen[base:base + slots, where:where + LANES], u), fan, slots)

    for c, nxt in zip(inv_copies, pass_copies[1:]):
        c.wait_recv()
        nxt.start()

    def first(b, _):
        at = pl.ds(pl.multiple_of(b * pair, pair), pair)
        multiply(b, y_ref[at, :].astype(BF16), False)
        return 0

    lax.fori_loop(0, slots, first, 0, unroll=64)

    row_lane = iota((slots, n_row * pad), 1).astype(F32)
    col_label = dot((kcol_c == row_lane).astype(BF16),
                    msg_ref[0:n_row * pad, half:half + LANES])
    own_lane = iota((slots, pad), 1).astype(F32)
    row_label = dot((krow_c == own_lane).astype(BF16), msg_ref[0:pad, half:half + LANES])
    marks = (col_label == iota((slots, LANES), 1).astype(F32)).astype(BF16)
    same_label = lax.dot_general(
        marks, marks, (((1,), (1,)), ((), ())), preferred_element_type=F32)
    same = jnp.where(group_c == group, same_label * keep_f, 0.0)
    panel = n_col * own
    dropped = jnp.where(
        iota((panel, slots), 0) == l_idx, jnp.broadcast_to(1.0 - keep_f, (panel, slots)), 0.0)
    sums = jnp.concatenate([same, dropped], axis=0)
    sums = jnp.concatenate([sums, sums], axis=1).astype(BF16)
    target = jnp.where(row_label == col_label, run_c, 0.0)[:, 0:pad]
    target = jnp.where(
        krow_c == (iota((slots, pad), 1) % own).astype(F32), target, 0.0).astype(BF16)

    grouped = []
    for u in range(chunk_b):
        high, low = split(collect(u, slots))
        r = dot(sums, jnp.concatenate([high, low], axis=0))
        lump_ref[:, u * LANES:(u + 1) * LANES] = r[slots:, :]
        grouped.append(r[:slots, :])

    lump_copies = [pltpu.make_async_remote_copy(
        src_ref=lump_ref.at[pl.ds(d * own, own)], dst_ref=in_ref.at[d],
        send_sem=ls.at[d], recv_sem=lr_.at[d],
        device_id=col_peer(d), device_id_type=MESH) for d in range(1, n_col)]
    for c in lump_copies:
        c.start()

    for u in range(chunk_b):
        spread((jnp.concatenate(split(grouped[u]), axis=1), u), fan2, slots)

    for c in pass_copies:
        c.wait_recv()

    inv_lane = iota((slots, n_col * pad), 1).astype(F32)
    pick = jnp.concatenate(
        [(inv_c == inv_lane).astype(BF16), (inv_c + own == inv_lane).astype(BF16)], axis=0)
    for t in range(half_a):
        r = dot(pick, inv_ref[:, t * LANES:(t + 1) * LANES])
        y_ref[pl.ds(t, slots, stride=chunk_a), :] = r[:slots]
        y_ref[pl.ds(t + half_a, slots, stride=chunk_a), :] = r[slots:]

    def second(b, _):
        at = pl.ds(pl.multiple_of(b * pair, pair), pair)
        multiply(b, y_ref[at, :].astype(BF16), True)
        return 0

    lax.fori_loop(0, slots, second, 0, unroll=64)
    for u in range(chunk_b):
        out_ref[:, u * LANES:(u + 1) * LANES] = collect(u, slots)

    for c in lump_copies:
        c.wait_recv()
    total = lump_ref[0:own, :]
    for d in range(1, n_col):
        total = total + in_ref[d]
    for u in range(chunk_b):
        spread((jnp.concatenate(split(total[:, u * LANES:(u + 1) * LANES]), axis=1), u),
               fan2, own)
    for e in range(own):
        multiply(e, tmp_ref[e * pair:(e + 1) * pair, :].astype(BF16), True)
    for u in range(chunk_b):
        at = slice(u * LANES, (u + 1) * LANES)
        out_ref[:, at] = out_ref[:, at] + dot(
            target, jnp.concatenate(split(collect(u, own)), axis=0))

    for c in copies + inv_copies + pass_copies + lump_copies:
        c.wait_send()


def body(a_blocks, blk_row, blk_col, drop_mask, prolong, agg_label, inv_diag):
    slots = a_blocks.shape[0]
    own = prolong.shape[0]
    n_row = lax.axis_size("row")
    n_col = lax.axis_size("col")
    wide = BS * PC
    vmem = pl.BlockSpec(memory_space=pltpu.VMEM)
    hbm = pl.BlockSpec(memory_space=pltpu.HBM)
    dma = pltpu.SemaphoreType.DMA
    return pl.pallas_call(
        functools.partial(kernel, n_row, n_col),
        out_shape=pltpu.VMEM((slots, wide), F32),
        in_specs=[hbm] * 7,
        out_specs=vmem,
        scratch_shapes=[
            pltpu.VMEM((1, slots), jnp.int32),
            pltpu.VMEM((1, slots), jnp.int32),
            pltpu.VMEM((1, slots), jnp.int32),
            pltpu.VMEM((1, own), jnp.int32),
            pltpu.VMEM(a_blocks.shape, BF16),
            pltpu.VMEM(prolong.shape, BF16),
            pltpu.VMEM(inv_diag.shape, BF16),
            pltpu.VMEM((slots * BS // 2, LANES), F32),
            pltpu.VMEM((slots * BS // 2, LANES), F32),
            pltpu.VMEM((slots * BS // 2, LANES), F32),
            pltpu.VMEM(((n_row + n_col - 1) * 2 * own, wide // 2 + LANES), BF16),
            pltpu.VMEM((n_col * 2 * own, BS * BS // 2), BF16),
            pltpu.VMEM((n_col * own, wide), F32),
            pltpu.VMEM((n_col, own, wide), F32),
            pltpu.VMEM((own * BS // 2, LANES), F32),
            dma((n_row,)), dma((n_row,)), dma((n_col,)), dma((n_col,)),
            dma((n_col,)), dma((n_col,)), dma((n_col,)), dma((n_col,)),
            dma((n_col,)), dma((n_col,)), dma((7,)),
        ],
        compiler_params=pltpu.CompilerParams(
            collective_id=0, has_side_effects=True, vmem_limit_bytes=56 * 2**20),
    )(
        blk_row.reshape(1, slots), blk_col.reshape(1, slots),
        drop_mask.reshape(1, slots), agg_label.reshape(1, own), a_blocks, prolong, inv_diag,
    )


def solution(mesh):
    return jax.shard_map(
        body,
        mesh=mesh,
        in_specs=(
            P(("row", "col"), None),
            P(("row", "col")),
            P(("row", "col")),
            P(("row", "col")),
            P(("row", "col"), None),
            P(("row", "col")),
            P(("row", "col"), None),
        ),
        out_specs=P(("row", "col"), None),
        check_vma=False,
    )
```

```python
import functools

import jax
import jax.numpy as jnp
from jax import lax
from jax.experimental import pallas as pl
from jax.experimental.pallas import tpu as pltpu
from jax.sharding import PartitionSpec as P

BS = 64
PC = 16
LANES = 128
MESH = pl.DeviceIdType.MESH
F32 = jnp.float32
BF16 = jnp.bfloat16


def iota(shape, dim):
    return lax.broadcasted_iota(jnp.int32, shape, dim)


def split(x):
    high = x.astype(BF16)
    return high, (x - high.astype(F32)).astype(BF16)


def dot(a, b):
    return jnp.dot(a, b, preferred_element_type=F32)


def kernel(
    n_row, n_col, row_hbm, col_hbm, drop_hbm, label_hbm, a_hbm, b_hbm, d_hbm,
    out_ref, row_ref, col_ref, drop_ref, label_ref, a_ref, b_ref, d_ref, y_ref, t_ref, s_ref, msg_ref, inv_ref, lump_ref, in_ref, tmp_ref,
    brs, brr, bcs, bcr, ds_, dr, fs, fr, ls, lr_, loads,
):
    slots = a_ref.shape[0]
    own = b_ref.shape[0]
    wide = BS * PC
    half = wide // 2
    pair = BS // 2
    chunk_a = BS * BS // LANES
    chunk_b = wide // LANES
    per_chunk = LANES // (2 * PC)
    pad = 2 * own
    me_row = lax.axis_index("row")
    me_col = lax.axis_index("col")

    def row_peer(d):
        return (lax.rem(me_row + d, n_row), me_col)

    def col_peer(d):
        return (me_row, lax.rem(me_col + d, n_col))

    fetch = [pltpu.make_async_copy(x, y, loads.at[i]) for i, (x, y) in enumerate((
        (d_hbm, d_ref), (b_hbm, b_ref), (label_hbm, label_ref), (row_hbm, row_ref),
        (col_hbm, col_ref), (drop_hbm, drop_ref), (a_hbm, a_ref)))]
    for c in fetch:
        c.start()
    partner = me_col + 1 - 2 * lax.rem(me_col, 2)

    barrier = pltpu.get_barrier_semaphore()
    for d in range(1, n_row):
        pl.semaphore_signal(barrier, inc=1, device_id=row_peer(d), device_id_type=MESH)
    for d in range(1, n_col):
        pl.semaphore_signal(barrier, inc=1, device_id=col_peer(d), device_id_type=MESH)

    fetch[1].wait()
    fetch[2].wait()
    b_all = b_ref[...]
    msg_ref[0:pad, 0:half] = jnp.concatenate([b_all[:, :half], b_all[:, half:]], axis=0)
    mine = (iota((pad, own), 0) == iota((pad, own), 1)).astype(F32)
    labels = jnp.sum(mine * label_ref[...].astype(F32), axis=1, keepdims=True)
    msg_ref[0:pad, half:half + LANES] = jnp.broadcast_to(labels, (pad, LANES)).astype(BF16)

    src = iota((LANES, LANES), 0)
    dst = iota((LANES, LANES), 1)
    want = dst // BS * BS + dst % pair * 2 + dst % BS // pair
    perm = (src == want).astype(BF16)
    half_a = chunk_a // 2
    fetch[0].wait()
    for t in range(half_a):
        pieces = [dot(d_ref[:, u * LANES:(u + 1) * LANES], perm) for u in (t, t + half_a)]
        tmp_ref[pl.ds(t, own, stride=chunk_a), :] = pieces[0]
        tmp_ref[pl.ds(t + half_a, own, stride=chunk_a), :] = pieces[1]
        inv_ref[0:pad, t * LANES:(t + 1) * LANES] = (
            jnp.concatenate(pieces, axis=0).astype(BF16))

    pl.semaphore_wait(barrier, n_row + n_col - 2)

    copies = []
    for d in range(1, n_row):
        copies.append(pltpu.make_async_remote_copy(
            src_ref=msg_ref.at[pl.ds(0, pad)], dst_ref=msg_ref.at[pl.ds(d * pad, pad)],
            send_sem=brs.at[d], recv_sem=brr.at[d],
            device_id=row_peer(d), device_id_type=MESH))
    for d in range(1, n_col):
        copies.append(pltpu.make_async_remote_copy(
            src_ref=msg_ref.at[pl.ds(0, pad), pl.ds(0, half)],
            dst_ref=msg_ref.at[pl.ds((n_row - 1 + d) * pad, pad), pl.ds(0, half)],
            send_sem=bcs.at[d], recv_sem=bcr.at[d],
            device_id=col_peer(d), device_id_type=MESH))
    half_col = n_col // 2
    inv_copies = [pltpu.make_async_remote_copy(
        src_ref=inv_ref.at[pl.ds(0, pad)], dst_ref=inv_ref.at[pl.ds(d * pad, pad)],
        send_sem=ds_.at[d], recv_sem=dr.at[d],
        device_id=col_peer(2 * d), device_id_type=MESH) for d in range(1, half_col)]
    pass_copies = [pltpu.make_async_remote_copy(
        src_ref=inv_ref.at[pl.ds(d * pad, pad)],
        dst_ref=inv_ref.at[pl.ds((half_col + d) * pad, pad)],
        send_sem=fs.at[d], recv_sem=fr.at[d],
        device_id=(me_row, partner), device_id_type=MESH) for d in range(half_col)]
    for c in copies:
        c.start()
    for c in inv_copies:
        c.start()
    pass_copies[0].start()

    fetch[6].wait()
    for t in range(chunk_a):
        y_ref[pl.ds(t, slots, stride=chunk_a), :] = dot(
            a_ref[:, t * LANES:(t + 1) * LANES], perm
        )

    for c in fetch[3:6]:
        c.wait()
    blk_row = row_ref[...]
    blk_col = col_ref[...]
    local = blk_row - me_row * (n_col * own)
    keep = jnp.maximum(drop_ref[...], (blk_row == blk_col).astype(jnp.int32))
    keep_f = keep.astype(F32)
    col_slot = lax.rem(me_row - blk_col // (n_col * own) + n_row, n_row)
    k_col = col_slot * pad + blk_col % own
    owner = local // own
    back = lax.rem(me_col - owner + n_col, n_col)
    away = lax.rem(partner - owner + n_col, n_col)
    held = jnp.where(back % 2 == 0, back // 2, half_col + away // 2)
    k_row = jnp.where(back == 0, 0, n_row - 1 + back) * pad + local % own
    l_idx = lax.rem(owner - me_col + n_col, n_col) * own + local % own
    same_run = (blk_col // own == blk_row // own).astype(F32)
    group = (local * n_row + col_slot).astype(F32)
    k_sel = jnp.where(keep == 1, k_col, k_row).astype(F32)
    sub = iota((8, slots), 0)
    packed = jnp.zeros((8, slots), F32)
    for at, v in enumerate((k_sel, k_col.astype(F32), k_row.astype(F32), group, same_run,
                            (held * pad + local % own).astype(F32))):
        packed = jnp.where(sub == at, v, packed)
    eye = (iota((slots, slots), 0) == iota((slots, slots), 1)).astype(F32)
    columns = lax.dot_general(
        eye, packed, (((1,), (1,)), ((), ())),
        precision=lax.Precision.HIGHEST, preferred_element_type=F32)
    sel_c, kcol_c, krow_c, group_c, run_c, inv_c = (
        columns[:, i:i + 1] for i in range(6))

    src = iota((LANES, per_chunk * LANES), 0)
    dst = iota((LANES, per_chunk * LANES), 1)
    fan = (src == dst // LANES * (2 * PC) + dst % (2 * PC)).astype(BF16)
    fan2 = jnp.concatenate([fan, fan], axis=0)
    lane = iota((pair, LANES), 1)
    even = lane // PC % 2 == 0

    def spread(x, fan, count):
        r = dot(x[0], fan)
        for v in range(per_chunk):
            t_ref[pl.ds(x[1] * per_chunk + v, count, stride=pair), :] = (
                r[:, v * LANES:(v + 1) * LANES])

    def multiply(b, lhs, two):
        at = pl.ds(pl.multiple_of(b * pair, pair), pair)
        g = t_ref[at, :]
        r = pltpu.roll(g, PC, 1)
        zero = jnp.zeros_like(g)
        parts = [jnp.where(even, g, zero), jnp.where(even, r, zero),
                 jnp.where(even, zero, r), jnp.where(even, zero, g)]
        x = jnp.concatenate(parts, axis=0)
        if two:
            high, low = split(x)
            s_ref[at, :] = dot(jnp.concatenate([lhs, lhs], axis=1),
                               jnp.concatenate([high, low], axis=0))
        else:
            s_ref[at, :] = dot(lhs, x.astype(BF16))

    def collect(u, count):
        place = iota((count, LANES), 1) // (2 * PC)
        z = s_ref[pl.ds(u * per_chunk, count, stride=pair), :]
        for v in range(1, per_chunk):
            z = jnp.where(
                place == v, s_ref[pl.ds(u * per_chunk + v, count, stride=pair), :], z)
        return z

    for c in copies:
        c.wait_recv()
    for c, nxt in zip(inv_copies, pass_copies[1:]):
        c.wait_recv()
        nxt.start()


    depth = msg_ref.shape[0]
    slot_lane = iota((slots, depth), 1).astype(F32)
    pick = jnp.concatenate(
        [(sel_c == slot_lane).astype(BF16), (sel_c + own == slot_lane).astype(BF16)], axis=0)
    chosen = dot(pick, msg_ref[:, 0:half]).astype(BF16)
    for u in range(chunk_b):
        where = u % (chunk_b // 2) * LANES
        base = u // (chunk_b // 2) * slots
        spread((chosen[base:base + slots, where:where + LANES], u), fan, slots)

    def first(b, _):
        at = pl.ds(pl.multiple_of(b * pair, pair), pair)
        multiply(b, y_ref[at, :].astype(BF16), False)
        return 0

    lax.fori_loop(0, slots, first, 0, unroll=64)

    row_lane = iota((slots, n_row * pad), 1).astype(F32)
    col_label = dot((kcol_c == row_lane).astype(BF16),
                    msg_ref[0:n_row * pad, half:half + LANES])
    own_lane = iota((slots, pad), 1).astype(F32)
    row_label = dot((krow_c == own_lane).astype(BF16), msg_ref[0:pad, half:half + LANES])
    marks = (col_label == iota((slots, LANES), 1).astype(F32)).astype(BF16)
    same_label = lax.dot_general(
        marks, marks, (((1,), (1,)), ((), ())), preferred_element_type=F32)
    same = jnp.where(group_c == group, same_label * keep_f, 0.0)
    panel = n_col * own
    dropped = jnp.where(
        iota((panel, slots), 0) == l_idx, jnp.broadcast_to(1.0 - keep_f, (panel, slots)), 0.0)
    sums = jnp.concatenate([same, dropped], axis=0)
    sums = jnp.concatenate([sums, sums], axis=1).astype(BF16)
    target = jnp.where(row_label == col_label, run_c, 0.0)[:, 0:pad]
    target = jnp.where(
        krow_c == (iota((slots, pad), 1) % own).astype(F32), target, 0.0).astype(BF16)

    grouped = []
    for u in range(chunk_b):
        high, low = split(collect(u, slots))
        r = dot(sums, jnp.concatenate([high, low], axis=0))
        lump_ref[:, u * LANES:(u + 1) * LANES] = r[slots:, :]
        grouped.append(r[:slots, :])

    lump_copies = [pltpu.make_async_remote_copy(
        src_ref=lump_ref.at[pl.ds(d * own, own)], dst_ref=in_ref.at[d],
        send_sem=ls.at[d], recv_sem=lr_.at[d],
        device_id=col_peer(d), device_id_type=MESH) for d in range(1, n_col)]
    for c in lump_copies:
        c.start()

    for u in range(chunk_b):
        spread((jnp.concatenate(split(grouped[u]), axis=1), u), fan2, slots)

    for c in pass_copies:
        c.wait_recv()

    inv_lane = iota((slots, n_col * pad), 1).astype(F32)
    pick = jnp.concatenate(
        [(inv_c == inv_lane).astype(BF16), (inv_c + own == inv_lane).astype(BF16)], axis=0)
    for t in range(half_a):
        r = dot(pick, inv_ref[:, t * LANES:(t + 1) * LANES])
        y_ref[pl.ds(t, slots, stride=chunk_a), :] = r[:slots]
        y_ref[pl.ds(t + half_a, slots, stride=chunk_a), :] = r[slots:]

    def second(b, _):
        at = pl.ds(pl.multiple_of(b * pair, pair), pair)
        multiply(b, y_ref[at, :].astype(BF16), True)
        return 0

    lax.fori_loop(0, slots, second, 0, unroll=64)
    for u in range(chunk_b):
        out_ref[:, u * LANES:(u + 1) * LANES] = collect(u, slots)

    for c in lump_copies:
        c.wait_recv()
    total = lump_ref[0:own, :]
    for d in range(1, n_col):
        total = total + in_ref[d]
    for u in range(chunk_b):
        spread((jnp.concatenate(split(total[:, u * LANES:(u + 1) * LANES]), axis=1), u),
               fan2, own)
    for e in range(own):
        multiply(e, tmp_ref[e * pair:(e + 1) * pair, :].astype(BF16), True)
    for u in range(chunk_b):
        at = slice(u * LANES, (u + 1) * LANES)
        out_ref[:, at] = out_ref[:, at] + dot(
            target, jnp.concatenate(split(collect(u, own)), axis=0))

    for c in copies + inv_copies + pass_copies + lump_copies:
        c.wait_send()


def body(a_blocks, blk_row, blk_col, drop_mask, prolong, agg_label, inv_diag):
    slots = a_blocks.shape[0]
    own = prolong.shape[0]
    n_row = lax.axis_size("row")
    n_col = lax.axis_size("col")
    wide = BS * PC
    vmem = pl.BlockSpec(memory_space=pltpu.VMEM)
    hbm = pl.BlockSpec(memory_space=pltpu.HBM)
    dma = pltpu.SemaphoreType.DMA
    return pl.pallas_call(
        functools.partial(kernel, n_row, n_col),
        out_shape=pltpu.VMEM((slots, wide), F32),
        in_specs=[hbm] * 7,
        out_specs=vmem,
        scratch_shapes=[
            pltpu.VMEM((1, slots), jnp.int32),
            pltpu.VMEM((1, slots), jnp.int32),
            pltpu.VMEM((1, slots), jnp.int32),
            pltpu.VMEM((1, own), jnp.int32),
            pltpu.VMEM(a_blocks.shape, BF16),
            pltpu.VMEM(prolong.shape, BF16),
            pltpu.VMEM(inv_diag.shape, BF16),
            pltpu.VMEM((slots * BS // 2, LANES), F32),
            pltpu.VMEM((slots * BS // 2, LANES), F32),
            pltpu.VMEM((slots * BS // 2, LANES), F32),
            pltpu.VMEM(((n_row + n_col - 1) * 2 * own, wide // 2 + LANES), BF16),
            pltpu.VMEM((n_col * 2 * own, BS * BS // 2), BF16),
            pltpu.VMEM((n_col * own, wide), F32),
            pltpu.VMEM((n_col, own, wide), F32),
            pltpu.VMEM((own * BS // 2, LANES), F32),
            dma((n_row,)), dma((n_row,)), dma((n_col,)), dma((n_col,)),
            dma((n_col,)), dma((n_col,)), dma((n_col,)), dma((n_col,)),
            dma((n_col,)), dma((n_col,)), dma((7,)),
        ],
        compiler_params=pltpu.CompilerParams(
            collective_id=0, has_side_effects=True, vmem_limit_bytes=56 * 2**20),
    )(
        blk_row.reshape(1, slots), blk_col.reshape(1, slots),
        drop_mask.reshape(1, slots), agg_label.reshape(1, own), a_blocks, prolong, inv_diag,
    )


def solution(mesh):
    return jax.shard_map(
        body,
        mesh=mesh,
        in_specs=(
            P(("row", "col"), None),
            P(("row", "col")),
            P(("row", "col")),
            P(("row", "col")),
            P(("row", "col"), None),
            P(("row", "col")),
            P(("row", "col"), None),
        ),
        out_specs=P(("row", "col"), None),
        check_vma=False,
    )
```
